256 devices in a mesh: dp: 4 (over y_hi, core), ctx: 64 (over z, y_lo, x).
Axes of the slice: x: 4, y: 4 (y_hi: 2, y_lo: 2; y = y_hi * 2 + y_lo), z: 8, core: 2. Of those that a mesh axis runs over, the one named last changes fastest.
Arguments:
- tokens: bfloat16 [4, 10240, 4096], P('dp', 'ctx'), may hold values from -6 to 6
- w_qkv: bfloat16 [4096, 5120], P('dp'), may hold values from -0.09375 to 0.09375
- col_scale: float32 [5120], replicated, may hold values from 0.4 to 1.6
- doc_ids: int32 [4, 10240], P('dp', 'ctx'), may hold values from 0 to 7, never falling along the last dimension, each value on 1 to 2560 neighbouring positions
Outputs:
- attended: bfloat16 [4, 10240, 4096], P('dp', 'ctx')
The draws below stay inside these ranges and needn't reach their ends.
Inputs may be any that keep to these rules, and one draw needn't show every extreme that they name: `doc_ids`: along each sequence the ids never fall; every document holds at most 2560 tokens and some document holds exactly 2560.
All inputs are finite; a program needn't handle non-finite values.
Results may differ from the reference program's by a relative error of at most 0.04.
Values may be sent and summed in bfloat16 or wider, within the bound.
A program may use at most 192 MiB of HBM per device.

```python
import math
import jax
import jax.numpy as jnp
import numpy as np
from jax import lax

D = 4096
QH = 32
KVH = 4
HD = 128
TOK_DEV = 160
BATCH = 4
SEQ_LEN = 10240
QKV = 5120
SPAN = 16
DOC_MAX = 2560
DOCS = 8
N_DP = 4


def draw_tokens(key, part):
    first = jax.random.fold_in(key, 0)
    base = jnp.clip(jax.random.normal(first, (BATCH, SEQ_LEN, D), jnp.float32), -6.0, 6.0)
    return base.astype(jnp.bfloat16)


def steps_of(own_key, extent, cuts, low, high):
    def one(axis_at, parts):
        steps = jax.random.uniform(jax.random.fold_in(jax.random.fold_in(own_key, 6), axis_at), (parts,), jnp.float32, low / len(cuts), high / len(cuts))
        return jnp.repeat(jnp.exp(steps), extent[axis_at] // parts).reshape((-1,) + (1,) * (len(extent) - axis_at - 1))

    level = one(*cuts[0])
    for cut in cuts[1:]:
        level = level * one(*cut)
    return level


def profile(count, total, bound, slope):
    loads = [(1 << 20) // math.isqrt(grade ** slope) + 1 for grade in range(2, count + 1)]
    spare, counts = total - bound - (count - 1), [1] * (count - 1)
    while spare > 0:
        movable = [i for i in range(count - 1) if counts[i] < bound]
        pool, budget = sum([loads[i] for i in movable]), spare
        for i in movable:
            addition = min(bound - counts[i], max(1, budget * loads[i] // pool), spare)
            counts[i] = counts[i] + addition
            spare = spare - addition
    return np.array([bound] + counts)


def uneven_parts(own_key, number_of, total, most, skew):
    if number_of == 2:
        one = jax.random.randint(own_key, (), max(1, total - most), min(most, total - 1) + 1)
        return jnp.stack([one, total - one])
    tallies = jnp.asarray(profile(number_of, total, most, skew), jnp.int32)
    pairs = (number_of - 1) // 2
    giver, taker = tallies[1:1 + 2 * pairs:2], tallies[2:2 + 2 * pairs:2]
    slack = jnp.minimum(giver - 1, most - taker)
    shifted = jax.random.randint(jax.random.fold_in(own_key, 1), (pairs,), 0, 1 << 20) % (slack + 1)
    tallies = tallies.at[1:1 + 2 * pairs:2].set(giver - shifted).at[2:2 + 2 * pairs:2].set(taker + shifted)
    return tallies[jax.random.permutation(jax.random.fold_in(own_key, 2), number_of)]


def gaussian(own_key, shape, scale, most, cuts=(), held_as=jnp.bfloat16):
    values = jax.random.normal(own_key, shape, jnp.float32) * scale
    if len(cuts) > 0:
        values = steps_of(own_key, shape, cuts, -0.22, 0.18) * values
    return jnp.clip(values, min=-most, max=most).astype(held_as)


def setup_inputs(seed: int = 0) -> dict:
    streams_of = jax.random.split(jax.random.key(seed), 5)
    return {
        "tokens": draw_tokens(jax.random.fold_in(streams_of[4], 71), 0),
        "w_qkv": gaussian(streams_of[1], (D, QKV), D ** -0.5, 0.09375, ((0, 4),)),
        "col_scale": jnp.clip(1.0 + 0.12 * jax.random.normal(streams_of[2], (QKV,), jnp.float32), 0.4, 1.6),
        "doc_ids": jax.vmap(lambda own: jnp.searchsorted(jnp.cumsum(uneven_parts(own, DOCS, SEQ_LEN, DOC_MAX, 2)), jnp.arange(SEQ_LEN), side="right"))(jax.random.split(streams_of[3], BATCH)).reshape((BATCH, SEQ_LEN)).astype(jnp.int32),
    }


def rotate(vectors, positions):
    half_width = vectors.shape[-1] // 2
    freqs = jnp.exp(-math.log(500000.0) * 2.0 * jnp.arange(half_width, dtype=jnp.float32) / vectors.shape[-1])
    angles = positions.astype(jnp.float32)[:, None] * freqs[None, :]
    cosine = jnp.cos(angles)[:, None, :]
    sine = jnp.sin(angles)[:, None, :]
    first = vectors[..., :half_width]
    second = vectors[..., half_width:]
    return jnp.concatenate([first * cosine - second * sine, second * cosine + first * sine], axis=-1)

def reference(tokens, w_qkv, col_scale, doc_ids):
    slice_rows = D // N_DP
    groups = QH // KVH
    padding = SPAN * TOK_DEV
    blocks = SEQ_LEN // TOK_DEV
    score_scale = 1.0 / math.sqrt(HD)

    def one_sequence(operands):
        features, documents = operands
        summed = jnp.zeros((SEQ_LEN, QKV), jnp.float32)
        for index in range(N_DP):
            term = jnp.dot(features[:, index * slice_rows:(index + 1) * slice_rows], w_qkv[index * slice_rows:(index + 1) * slice_rows], preferred_element_type=jnp.float32)
            term = lax.optimization_barrier(term.astype(jnp.bfloat16)).astype(jnp.float32)
            summed = summed + term
        qkv = summed * col_scale
        positions = jnp.arange(SEQ_LEN, dtype=jnp.int32)
        queries = rotate(qkv[:, :QH * HD].reshape(SEQ_LEN, QH, HD), positions).astype(jnp.bfloat16)
        keys = rotate(qkv[:, QH * HD:(QH + KVH) * HD].reshape(SEQ_LEN, KVH, HD), positions).astype(jnp.bfloat16)
        values = qkv[:, (QH + KVH) * HD:].reshape(SEQ_LEN, KVH, HD).astype(jnp.bfloat16)
        keys_padded = jnp.concatenate([jnp.zeros((padding, KVH, HD), jnp.bfloat16), keys], axis=0)
        values_padded = jnp.concatenate([jnp.zeros((padding, KVH, HD), jnp.bfloat16), values], axis=0)
        docs_padded = jnp.concatenate([jnp.full((padding,), -1, jnp.int32), documents.astype(jnp.int32)], axis=0)
        pos_padded = jnp.concatenate([jnp.arange(-padding, 0, dtype=jnp.int32), positions], axis=0)

        def one_block(index):
            start = (index * TOK_DEV).astype(jnp.int32)
            query_rows = lax.dynamic_slice_in_dim(queries, start, TOK_DEV, 0).reshape(TOK_DEV, KVH, groups, HD)
            query_pos = lax.dynamic_slice_in_dim(positions, start, TOK_DEV, 0)
            query_docs = lax.dynamic_slice_in_dim(documents.astype(jnp.int32), start, TOK_DEV, 0)
            key_rows = lax.dynamic_slice_in_dim(keys_padded, start, padding + TOK_DEV, 0)
            value_rows = lax.dynamic_slice_in_dim(values_padded, start, padding + TOK_DEV, 0)
            key_docs = lax.dynamic_slice_in_dim(docs_padded, start, padding + TOK_DEV, 0)
            key_pos = lax.dynamic_slice_in_dim(pos_padded, start, padding + TOK_DEV, 0)
            mask = (key_docs[None, :] == query_docs[:, None]) & (key_pos[None, :] <= query_pos[:, None]) & (key_pos[None, :] >= 0)
            scores = jnp.einsum('tgjd,sgd->gjts', query_rows.astype(jnp.float32), key_rows.astype(jnp.float32)) * score_scale
            scores = jnp.where(mask[None, None], scores, -jnp.inf)
            row_max = lax.optimization_barrier(jnp.max(scores, axis=-1))
            expo = jnp.exp(scores - row_max[..., None])
            total = lax.optimization_barrier(jnp.sum(expo, axis=-1))
            weights = lax.optimization_barrier(expo.astype(jnp.bfloat16)).astype(jnp.float32)
            mixed = jnp.einsum('gjts,sgd->gjtd', weights, value_rows.astype(jnp.float32)) / total[..., None]
            return mixed.transpose(2, 0, 1, 3).reshape(TOK_DEV, QH * HD).astype(jnp.bfloat16)
        result = lax.map(one_block, jnp.arange(blocks, dtype=jnp.int32))
        return result.reshape(SEQ_LEN, QH * HD)
    return lax.map(one_sequence, (tokens, doc_ids))
```

```python
import math

import jax
import jax.numpy as jnp
from jax import lax
from jax.experimental import pallas as pl
from jax.experimental.pallas import tpu as pltpu
from jax.sharding import PartitionSpec as P

MESH = pl.DeviceIdType.MESH
QH = 32
KVH = 4
HD = 128
T = 160
SLICE = 1024
CH = 512
NCH = 10
SPAN = 16
BLK = 2 * T + 16
F32 = jnp.float32
BF16 = jnp.bfloat16


def project_kernel(
    tok, w, scale, cosf, sinf, docs,
    q_out, kv,
    wv, xo, xp, po, p1, sso, rso, ssp, rsp, sx, rx, own,
    w_sem, loc_sem, tok_s, tok_r, sso_s, sso_r, ssp_s, ssp_r, sx_s, sx_r, h_s, h_r, h_r2,
):
    dp = lax.axis_index("dp")
    ctx = lax.axis_index("ctx")
    h = dp // 2
    k = dp % 2
    z = ctx // 8
    b = (ctx // 4) % 2
    x = ctx % 4

    def place(h_, k_, z_, b_, x_):
        return (h_ * 2 + k_, z_ * 8 + b_ * 4 + x_)

    sib = place(h, 1 - k, z, b, x)
    par = place(1 - h, k, z, 1 - b, x)
    parx = place(1 - h, 1 - k, z, 1 - b, x)
    z_up = place(h, k, (z + 1) % 8, b, x)
    z_dn = place(h, k, (z + 7) % 8, b, x)
    xi, xm, x2 = (x + 1) % 4, (x + 3) % 4, (x + 2) % 4
    d_i = place(h, k, z, b, xi)
    d_m = place(h, k, z, b, xm)
    d_2 = place(h, k, z, b, x2)
    d_y = place(h, k, z, 1 - b, x)

    def cols(i):
        return pl.ds(pl.multiple_of(((i + 8) % 10) * CH, CH), CH)

    def tok_cols(j):
        return pl.ds(pl.multiple_of(j * SLICE, SLICE), SLICE)

    def w_copy(i):
        return pltpu.make_async_copy(w.at[:, cols(i)], wv.at[i], w_sem.at[i])

    own_tok = pltpu.make_async_copy(tok.at[:, tok_cols(2 * h + k)], xo.at[pl.ds(0, T)], loc_sem.at[0])
    own_tok.start()
    for i in range(NCH):
        w_copy(i).start()

    bar = pltpu.get_barrier_semaphore()
    for dev in (sib, par, parx, z_dn, d_i, d_m, d_2, d_y):
        pl.semaphore_signal(bar, inc=1, device_id=dev, device_id_type=MESH)
    pl.semaphore_wait(bar, 8)

    def remote(src, dst, s, r, dev):
        return pltpu.make_async_remote_copy(
            src_ref=src, dst_ref=dst, send_sem=s, recv_sem=r, device_id=dev, device_id_type=MESH
        )

    t_par = remote(tok.at[:, tok_cols(2 * (1 - h) + k)], xp.at[pl.ds(0, T)], tok_s.at[0], tok_r.at[0], par)
    t_parx = remote(tok.at[:, tok_cols(2 * (1 - h) + 1 - k)], xp.at[pl.ds(T, T)], tok_s.at[1], tok_r.at[1], parx)
    t_sib = remote(tok.at[:, tok_cols(2 * h + 1 - k)], xo.at[pl.ds(T, T)], tok_s.at[2], tok_r.at[2], sib)
    t_par.start()
    t_parx.start()
    t_sib.start()

    own_tok.wait()
    t_sib.wait_recv()

    def sso_copy(i):
        return remote(sso.at[i], rso.at[i], sso_s.at[i], sso_r.at[i], sib)

    def ssp_copy(i):
        return remote(ssp.at[i], rsp.at[i], ssp_s.at[i], ssp_r.at[i], sib)

    def sx_copy(i):
        return remote(sx.at[i], rx.at[i], sx_s.at[i], sx_r.at[i], par)

    def own_part(i, c):
        w_copy(i).wait()
        part = jnp.dot(xo[...], wv[i], preferred_element_type=F32)
        po[i] = part[:T]
        sso[i] = part[T:].astype(BF16)
        sso_copy(i).start()
        return c

    lax.fori_loop(0, NCH, own_part, 0)

    t_par.wait_recv()
    t_parx.wait_recv()

    def partner_part(i, c):
        @pl.when(i < NCH)
        def _():
            part = jnp.dot(xp[...], wv[i], preferred_element_type=F32)
            p1[i] = part[:T].astype(BF16)
            ssp[i] = part[T:].astype(BF16)
            ssp_copy(i).start()

        @pl.when(i > 0)
        def _():
            ssp_copy(i - 1).wait_recv()
            sx[i - 1] = (p1[i - 1].astype(F32) + rsp[i - 1].astype(F32)).astype(BF16)
            sx_copy(i - 1).start()

        return c

    lax.fori_loop(0, NCH + 1, partner_part, 0)

    def summed(i):
        sso_copy(i).wait_recv()
        sx_copy(i).wait_recv()
        return (po[i] + rso[i].astype(F32) + rx[i].astype(F32)) * scale[(i + 8) % 10]

    def turned(u):
        return u * cosf[...] + pltpu.roll(u, HD // 2, 1) * sinf[...]

    own[pl.ds(2 * T, 16), :] = jnp.zeros((16, CH), BF16)
    own[pl.ds(2 * T, 16), pl.ds(0, T)] = jnp.broadcast_to(docs[...].astype(F32), (16, T)).astype(BF16)
    u = summed(0)
    for g in range(KVH):
        own[pl.ds(0, T), g * HD:(g + 1) * HD] = turned(u[:, g * HD:(g + 1) * HD]).astype(BF16)
    own[pl.ds(T, T), :] = summed(1).astype(BF16)

    put_own = pltpu.make_async_copy(own, kv.at[SPAN], loc_sem.at[1])
    put_own.start()

    K_ROWS = (0, T)
    V_ROWS = (T, T + 16)
    ALL = (0, BLK)

    def send(n, src, o, dist, dev, rows=ALL, sem=None):
        sem = h_r if sem is None else sem
        at = pl.ds(rows[0], rows[1])
        src = own if src else kv.at[SPAN - o]
        return remote(src.at[at], kv.at[SPAN - o - dist, at], h_s.at[n], sem.at[SPAN - o - dist], dev)

    def arrive(o, rows=ALL, sem=None):
        sem = h_r if sem is None else sem
        at = pl.ds(rows[0], rows[1])
        remote(kv.at[SPAN - o, at], kv.at[SPAN - o, at], h_s.at[0], sem.at[SPAN - o], sib).wait_recv()

    def late(v):
        return v < x

    ydist = 4 - 8 * b

    def y_first(n):
        return send(n, True, 0, ydist, d_y)

    def y_last(n):
        return send(n, False, 16, ydist, d_y)

    row = ((3, xi, d_i), (4, xm, d_m), (5, x2, d_2))

    z1 = send(0, True, 0, 8, z_up)
    z1.start()

    @pl.when(b == 0)
    def _():
        y_first(2).start()

    for n, v, dev in row:
        @pl.when(v > x)
        def _():
            send(n, True, 0, v - x, dev).start()

    def finish_q(i, c):
        u = summed(i)
        for g in range(CH // HD):
            at = pl.multiple_of((i - 2) * CH + g * HD, HD)
            q_out[:, pl.ds(at, HD)] = turned(u[:, g * HD:(g + 1) * HD]).astype(BF16)
        return c

    def finish(lo, hi):
        lax.fori_loop(lo, hi, finish_q, 0)

    finish(2, 4)
    arrive(8)
    z2 = send(1, False, 8, 8, z_up)
    a_i = send(6, False, 8, xi - x, d_i)
    a_m = send(7, False, 8, xm - x, d_m)
    a_y = send(8, False, 8, ydist, d_y)
    z2.start()
    a_i.start()
    a_m.start()
    a_y.start()

    yo = jnp.where(b == 1, 4, 12)

    def spread_start():
        arrive(yo)
        send(14, False, yo, xi - x, d_i).start()
        send(15, False, yo, xm - x, d_m).start()

    def spread_on():
        arrive(yo + x - xm)
        send(16, False, yo + x - xm, xi - x, d_i, K_ROWS).start()
        arrive(yo + x - xi)
        send(17, False, yo + x - xi, xm - x, d_m, V_ROWS, h_r2).start()

    finish(4, 5)

    @pl.when(b == 1)
    def _():
        spread_start()

    arrive(8 + x - xm)
    fa_i = send(9, False, 8 + x - xm, xi - x, d_i, K_ROWS)
    fa_y1 = send(10, False, 8 + x - xm, ydist, d_y)
    fa_i.start()
    fa_y1.start()
    arrive(8 + x - xi)
    fa_m = send(11, False, 8 + x - xi, xm - x, d_m, V_ROWS, h_r2)
    fa_y2 = send(12, False, 8 + x - xi, ydist, d_y)
    fa_m.start()
    fa_y2.start()
    finish(5, 6)

    arrive(16)
    for n, v, dev in row:
        @pl.when(v < x)
        def _():
            send(n, False, 16, v - x, dev).start()

    @pl.when(b == 1)
    def _():
        y_last(2).start()

    arrive(8 + x - x2, K_ROWS)
    arrive(8 + x - x2, V_ROWS, h_r2)
    fa_y3 = send(13, False, 8 + x - x2, ydist, d_y)
    fa_y3.start()

    @pl.when(b == 1)
    def _():
        spread_on()

    finish(6, 8)

    @pl.when(b == 0)
    def _():
        spread_start()

    finish(8, 9)

    @pl.when(b == 0)
    def _():
        spread_on()

    finish(9, 10)

    arrive(yo + x - x2, K_ROWS)
    arrive(yo + x - x2, V_ROWS, h_r2)
    for v in (xi, xm, x2):
        d = x - v
        arrive(jnp.where(d > 0, d, 16 + d))
    for v in (x, xi, xm, x2):
        arrive(8 - ydist + x - v)

    put_own.wait()
    t_par.wait_send()
    t_parx.wait_send()
    t_sib.wait_send()

    def sent(i, c):
        sso_copy(i).wait_send()
        ssp_copy(i).wait_send()
        sx_copy(i).wait_send()
        return c

    lax.fori_loop(0, NCH, sent, 0)
    for n in (0, 1, 2, 3, 4, 5, 6, 7, 8, 10, 12, 13, 14, 15):
        send(n, True, 0, 8, z_up).wait_send()
    for n in (9, 16):
        send(n, True, 0, 8, z_up, K_ROWS).wait_send()
    for n in (11, 17):
        send(n, True, 0, 8, z_up, V_ROWS).wait_send()


def project(tok, w, scale, cosf, sinf, docs):
    vmem = pl.BlockSpec(memory_space=pltpu.VMEM)
    hbm = pl.BlockSpec(memory_space=pl.ANY)
    chunks = pltpu.VMEM((NCH, T, CH), BF16)
    dma = pltpu.SemaphoreType.DMA
    return pl.pallas_call(
        project_kernel,
        out_shape=(
            jax.ShapeDtypeStruct((T, QH * HD), BF16),
            jax.ShapeDtypeStruct((SPAN + 1, BLK, CH), BF16),
        ),
        in_specs=[hbm, hbm, vmem, vmem, vmem, vmem],
        out_specs=(vmem, hbm),
        scratch_shapes=[
            pltpu.VMEM((NCH, SLICE, CH), BF16),
            pltpu.VMEM((2 * T, SLICE), BF16),
            pltpu.VMEM((2 * T, SLICE), BF16),
            pltpu.VMEM((NCH, T, CH), F32),
            chunks, chunks, chunks, chunks, chunks, chunks, chunks,
            pltpu.VMEM((BLK, CH), BF16),
            dma((NCH,)), dma((2,)), dma((3,)), dma((3,)),
            dma((NCH,)), dma((NCH,)), dma((NCH,)), dma((NCH,)), dma((NCH,)), dma((NCH,)),
            dma((18,)), dma((SPAN + 1,)), dma((SPAN + 1,)),
        ],
        compiler_params=pltpu.CompilerParams(
            collective_id=0, has_side_effects=True, vmem_limit_bytes=56 << 20
        ),
        name="project",
    )(tok, w, scale, cosf, sinf, docs)


def attend_kernel(q, kv, docs, out, keys, values, key_docs, bias, sem):
    k_copy = pltpu.make_async_copy(kv.at[:, pl.ds(0, T)], keys, sem.at[0])
    v_copy = pltpu.make_async_copy(kv.at[:, pl.ds(T, T)], values, sem.at[1])
    d_copy = pltpu.make_async_copy(kv.at[:, pl.ds(2 * T, 16)], key_docs, sem.at[2])
    d_copy.start()
    k_copy.start()
    v_copy.start()
    n_keys = (SPAN + 1) * T
    ctx = lax.axis_index("ctx")
    mine = docs[...].astype(F32)
    d_copy.wait()
    start = jnp.zeros((T, 1), F32)
    for i in range(SPAN + 1):
        theirs = key_docs[i, 0:1, 0:T].astype(F32)
        if i == SPAN:
            start += jnp.sum((theirs < mine).astype(F32), axis=1, keepdims=True)
        else:
            valid = (ctx >= SPAN - i).astype(F32)
            start -= valid * jnp.sum((theirs == mine).astype(F32), axis=1, keepdims=True)
    at = lax.broadcasted_iota(jnp.int32, (T, n_keys), 1).astype(F32) - float(SPAN * T)
    t = lax.broadcasted_iota(jnp.int32, (T, n_keys), 0).astype(F32)
    bias[...] = jnp.where((at >= start) & (at <= t), 0.0, -jnp.inf)
    k_copy.wait()
    v_copy.wait()
    factor = math.log2(math.e) / math.sqrt(HD)
    group = QH // KVH

    for g in range(KVH):
        kg = keys[:, :, g * HD:(g + 1) * HD].reshape(n_keys, HD)
        vg = values[:, :, g * HD:(g + 1) * HD].reshape(n_keys, HD)

        def head(j, c):
            cols = pl.ds(pl.multiple_of((g * group + j) * HD, HD), HD)
            s = lax.dot_general(q[:, cols], kg, (((1,), (1,)), ((), ())), preferred_element_type=F32)
            s = s + bias[...]
            m = jnp.max(s, axis=1, keepdims=True)
            p = jnp.exp2((s - m) * factor)
            total = jnp.sum(p, axis=1, keepdims=True)
            o = jnp.dot(p.astype(BF16), vg, preferred_element_type=F32)
            out[:, cols] = (o / total).astype(BF16)
            return c

        lax.fori_loop(0, group, head, 0)


def attend(q, kv, docs):
    vmem = pl.BlockSpec(memory_space=pltpu.VMEM)
    n = SPAN + 1
    return pl.pallas_call(
        attend_kernel,
        out_shape=jax.ShapeDtypeStruct((T, QH * HD), BF16),
        in_specs=[vmem, pl.BlockSpec(memory_space=pl.ANY), vmem],
        out_specs=vmem,
        scratch_shapes=[
            pltpu.VMEM((n, T, CH), BF16),
            pltpu.VMEM((n, T, CH), BF16),
            pltpu.VMEM((n, 16, CH), BF16),
            pltpu.VMEM((T, n * T), F32),
            pltpu.SemaphoreType.DMA((3,)),
        ],
        compiler_params=pltpu.CompilerParams(vmem_limit_bytes=56 << 20),
        name="attend",
    )(q, kv, docs)


def local(tokens, w_qkv, col_scale, doc_ids):
    positions = lax.axis_index("ctx") * T + jnp.arange(T, dtype=jnp.int32)
    half = HD // 2
    freqs = jnp.exp(-math.log(500000.0) * 2.0 * jnp.arange(half, dtype=F32) / HD)
    angles = positions.astype(F32)[:, None] * freqs[None, :]
    cosine, sine = jnp.cos(angles), jnp.sin(angles)
    cosf = jnp.concatenate([cosine, cosine], axis=1)
    sinf = jnp.concatenate([-sine, sine], axis=1)
    q, kv = project(
        tokens[0], w_qkv, col_scale.reshape(NCH, 1, CH), cosf, sinf, doc_ids
    )
    out = attend(q, kv, doc_ids.reshape(T, 1))
    return out[None]


def solution(mesh):
    return jax.shard_map(
        local,
        mesh=mesh,
        in_specs=(P("dp", "ctx", None), P("dp", None), P(), P("dp", "ctx")),
        out_specs=P("dp", "ctx", None),
        check_vma=False,
    )
```

```python
import math

import jax
import jax.numpy as jnp
from jax import lax
from jax.experimental import pallas as pl
from jax.experimental.pallas import tpu as pltpu
from jax.sharding import PartitionSpec as P

MESH = pl.DeviceIdType.MESH
QH = 32
KVH = 4
HD = 128
T = 160
H = T // 2
SLICE = 1024
CH = 512
NCH = 10
NQ = 8
PER = CH // HD
BLK = 2 * T + 16
AT = ((0, T + 16), (T + 16, T))
IDS = T
NPOS = 17
FIRST = 9
F32 = jnp.float32
BF16 = jnp.bfloat16
FACTOR = math.log2(math.e) / math.sqrt(HD)


def fused_kernel(
    tok, w, scale, cosf, sinf, docs, docs_col,
    out,
    wv, xo, xp, po, p1, sso, rso, ssp, rsp, sx, rx, kp1, kss, krs, ksx, krx, kv, q, acc, top, bias1, bias2,
    w_sem, loc_sem, tok_s, tok_r, sso_s, sso_r, ssp_s, ssp_r, sx_s, sx_r, kss_s, kss_r, ksx_s, ksx_r, h_s, h_r,
):
    dp = lax.axis_index("dp")
    ctx = lax.axis_index("ctx")
    h = dp // 2
    k = dp % 2
    z = ctx // 8
    b = (ctx // 4) % 2
    x = ctx % 4

    def place(h_, k_, z_, b_, x_):
        return (h_ * 2 + k_, z_ * 8 + b_ * 4 + x_)

    sib = place(h, 1 - k, z, b, x)
    par = place(1 - h, k, z, 1 - b, x)
    parx = place(1 - h, 1 - k, z, 1 - b, x)
    z_up = place(h, k, (z + 1) % 8, b, x)
    z_dn = place(h, k, (z + 7) % 8, b, x)
    xi, xm, x2 = (x + 1) % 4, (x + 3) % 4, (x + 2) % 4
    d_i = place(h, k, z, b, xi)
    d_m = place(h, k, z, b, xm)
    d_2 = place(h, k, z, b, x2)
    d_y = place(h, k, z, 1 - b, x)

    def cols(i):
        return pl.ds(pl.multiple_of(((i + 8) % 10) * CH, CH), CH)

    def tok_cols(j):
        return pl.ds(pl.multiple_of(j * SLICE, SLICE), SLICE)

    def w_copy(i):
        return pltpu.make_async_copy(w.at[:, cols(i)], wv.at[i], w_sem.at[i])

    def remote(src, dst, s, r, dev):
        return pltpu.make_async_remote_copy(
            src_ref=src, dst_ref=dst, send_sem=s, recv_sem=r, device_id=dev, device_id_type=MESH
        )

    own_tok = pltpu.make_async_copy(tok.at[:, tok_cols(2 * h + k)], xo.at[pl.ds(0, T)], loc_sem.at[0])
    own_tok.start()
    for i in range(NCH):
        w_copy(i).start()

    bar = pltpu.get_barrier_semaphore()
    for dev in (sib, par, parx, z_dn, d_i, d_m, d_2, d_y):
        pl.semaphore_signal(bar, inc=1, device_id=dev, device_id_type=MESH)
    pl.semaphore_wait(bar, 8)

    def tok_copy(f, far):
        j = 2 * (1 - h) + (1 - k if far else k)
        n = 2 * f + far
        return remote(
            tok.at[pl.ds(f * H, H), tok_cols(j)], xp.at[f, pl.ds(far * H, H)], tok_s.at[n], tok_r.at[n],
            parx if far else par,
        )

    t_sib = remote(tok.at[:, tok_cols(2 * h + 1 - k)], xo.at[pl.ds(T, T)], tok_s.at[4], tok_r.at[4], sib)
    tok_copy(0, 0).start()
    tok_copy(0, 1).start()
    t_sib.start()
    own_tok.wait()
    t_sib.wait_recv()

    def sso_copy(i):
        return remote(sso.at[i], rso.at[i], sso_s.at[i], sso_r.at[i], sib)

    def ssp_copy(i):
        return remote(ssp.at[i], rsp.at[i], ssp_s.at[i], ssp_r.at[i], sib)

    def sx_copy(i):
        return remote(sx.at[i], rx.at[i], sx_s.at[i], sx_r.at[i], par)

    def kss_copy(f):
        return remote(kss.at[f], krs.at[f], kss_s.at[f], kss_r.at[f], sib)

    def ksx_copy(f):
        return remote(ksx.at[f], krx.at[f], ksx_s.at[f], ksx_r.at[f], par)

    def own_part(i, c):
        w_copy(i).wait()
        part = jnp.dot(xo[...], wv[i], preferred_element_type=F32)
        po[i] = part[:T]
        sso[i] = part[T:].astype(BF16)
        sso_copy(i).start()
        return c

    lax.fori_loop(0, 6, own_part, 0)
    for far in range(2):
        tok_copy(0, far).wait_send()
        tok_copy(1, far).start()
    lax.fori_loop(6, NCH, own_part, 0)

    def kv_part(f):
        for far in range(2):
            tok_copy(f, far).wait_recv()
        for i in range(2):
            part = jnp.dot(xp[f], wv[i], preferred_element_type=F32)
            kp1[:, i * CH:(i + 1) * CH] = part[:H]
            kss[f, :, i * CH:(i + 1) * CH] = part[H:].astype(BF16)
        kss_copy(f).start()
        kss_copy(f).wait_recv()
        ksx[f] = (kp1[...] + krs[f].astype(F32)).astype(BF16)
        ksx_copy(f).start()

    def turned(u, rows):
        return u * cosf[rows, :] + pltpu.roll(u, HD // 2, 1) * sinf[rows, :]

    def kv_final(f):
        rows = pl.ds(f * H, H)
        at = AT[f][0]
        ksx_copy(f).wait_recv()
        if f == 0:
            for i in range(2):
                sso_copy(i).wait_recv()
        u = (po[0, rows] + rso[0, rows].astype(F32) + krx[f, :, :CH].astype(F32)) * scale[8]
        for g in range(KVH):
            kv[0, pl.ds(at, H), g * HD:(g + 1) * HD] = turned(u[:, g * HD:(g + 1) * HD], rows).astype(BF16)
        u = (po[1, rows] + rso[1, rows].astype(F32) + krx[f, :, CH:].astype(F32)) * scale[9]
        kv[0, pl.ds(at + H, H), :] = u.astype(BF16)

    def q_part(i, c):
        part = jnp.dot(xp[...].reshape(2 * T, SLICE), wv[i], preferred_element_type=F32)
        p1[i] = jnp.concatenate([part[:H], part[2 * H:3 * H]], axis=0).astype(BF16)
        ssp[i] = jnp.concatenate([part[H:2 * H], part[3 * H:]], axis=0).astype(BF16)
        ssp_copy(i).start()

        @pl.when(i > 2)
        def _():
            q_sum(i - 1)

        return c

    def q_sum(i):
        ssp_copy(i).wait_recv()
        sx[i] = (p1[i].astype(F32) + rsp[i].astype(F32)).astype(BF16)
        sx_copy(i).start()

    def q_parts(lo, hi):
        lax.fori_loop(lo, hi, q_part, 0)

    def q_final(i):
        sso_copy(i).wait_recv()
        sx_copy(i).wait_recv()
        u = (po[i] + rso[i].astype(F32) + rx[i].astype(F32)) * (scale[(i + 8) % 10] * FACTOR)
        for g in range(PER):
            q[i - 2, :, g * HD:(g + 1) * HD] = turned(u[:, g * HD:(g + 1) * HD], pl.ds(0, T)).astype(BF16)

    ya = FIRST + 4 * b
    yb = FIRST + 4 * (1 - b)
    ya_there = FIRST + 4 * (1 - b)
    yb_there = FIRST + 4 * b

    def send(n, f, src, dst, dev):
        at = pl.ds(AT[f][0], AT[f][1])
        return remote(kv.at[src, at], kv.at[dst, at], h_s.at[f, n], h_r.at[f, dst], dev)

    def arrive(f, dst):
        at = pl.ds(AT[f][0], AT[f][1])
        remote(kv.at[dst, at], kv.at[dst, at], h_s.at[f, 0], h_r.at[f, dst], sib).wait_recv()

    row = ((9, xi, 6, d_i), (10, xm, 7, d_m), (11, x2, 8, d_2))

    def near_start(f):
        send(0, f, 0, 1, z_up).start()

        @pl.when(b == 0)
        def _():
            send(12, f, 0, yb_there, d_y).start()

        for n, v, dst, dev in row:
            @pl.when(v > x)
            def _():
                send(n, f, 0, dst, dev).start()

    def plane_start(f):
        arrive(f, 1)
        send(1, f, 1, 2, z_up).start()
        send(2, f, 1, 3, d_i).start()
        send(3, f, 1, 4, d_m).start()
        send(4, f, 1, ya_there, d_y).start()

    def plane_on(f):
        arrive(f, 3)
        if f == 0:
            send(5, f, 3, 5, d_i).start()
        send(6, f, 3, ya_there + 1, d_y).start()
        arrive(f, 4)
        if f == 1:
            send(5, f, 4, 5, d_m).start()
        send(7, f, 4, ya_there + 2, d_y).start()

    def plane_last(f):
        arrive(f, 5)
        send(8, f, 5, ya_there + 3, d_y).start()

    def far_start(f):
        arrive(f, 2)

        @pl.when(b == 1)
        def _():
            send(12, f, 2, yb_there, d_y).start()

        for n, v, dst, dev in row:
            @pl.when(v < x)
            def _():
                send(n, f, 2, dst, dev).start()

    def spread_start(f, which):
        @pl.when(b == which)
        def _():
            arrive(f, yb)
            send(13, f, yb, yb + 1, d_i).start()
            send(14, f, yb, yb + 2, d_m).start()

    def spread_on(f, which):
        @pl.when(b == which)
        def _():
            if f == 0:
                arrive(f, yb + 2)
                send(15, f, yb + 2, yb + 3, d_m).start()
            else:
                arrive(f, yb + 1)
                send(15, f, yb + 1, yb + 3, d_i).start()

    def ya_rest():
        for r in range(4):
            for f in range(2):
                arrive(f, ya + r)

    def yb_rest():
        arrive(0, yb + 1)
        arrive(1, yb + 2)
        for f in range(2):
            arrive(f, yb + 3)

    ydist = 4 - 8 * b
    yo = jnp.where(b == 1, 4, 12)
    away = [jnp.int32(0), jnp.int32(8), jnp.int32(16), 8 + x - xm, 8 + x - xi, 8 + x - x2]
    away += [jnp.where(v < x, x - v, 16 + x - v) for v in (xm, xi, x2)]
    cross_b = [yo + x - v for v in (x, xm, xi, x2)]
    cross_a = [8 - ydist + x - v for v in (x, xm, xi, x2)]
    away += [jnp.where(b == 1, m, n) for m, n in zip(cross_b, cross_a)]
    away += [jnp.where(b == 1, n, m) for m, n in zip(cross_b, cross_a)]

    def make_bias(ref, p0, n):
        mine = docs_col[...].astype(F32)
        col = lax.broadcasted_iota(jnp.int32, (1, n * T), 1).astype(F32)
        seg = jnp.floor((col + 0.5) / H)
        second = seg >= n
        pos = jnp.where(second, seg - n, seg)
        r = col - H * seg + jnp.where(second, float(H), 0.0)
        low = jnp.zeros((T, n * T), F32)
        for i in range(n):
            ids = kv[p0 + i, pl.ds(IDS, 16), :][0:1, 0:T].astype(F32)
            count = jnp.sum((ids < mine).astype(F32), axis=1, keepdims=True)
            count = jnp.where(ctx >= away[p0 + i], count, float(T))
            low = jnp.where(pos == i, count, low)
        keep = r >= low
        if p0 == 0:
            t = lax.broadcasted_iota(jnp.int32, (T, n * T), 0).astype(F32)
            keep = keep & ((pos > 0.0) | (r <= t))
        ref[...] = jnp.where(keep, 0.0, -jnp.inf)

    def attend(i, p0, n, bias, last):
        g = i // 2
        lanes = pl.ds(pl.multiple_of(g * HD, HD), HD)
        where = pl.ds(p0, n)

        def rows(lo):
            parts = [kv[where, pl.ds(AT[f][0] + lo, H), lanes].reshape(n * H, HD) for f in range(2)]
            return jnp.concatenate(parts, axis=0)

        keys = rows(0)
        vals = jnp.concatenate([rows(H), jnp.ones((n * T, HD), BF16)], axis=1)
        for j in range(PER):
            qj = q[i, :, j * HD:(j + 1) * HD]
            s = lax.dot_general(qj, keys, (((1,), (1,)), ((), ())), preferred_element_type=F32) + bias[...]
            m = jnp.max(s, axis=1, keepdims=True)
            if p0 > 0:
                before = top[i, j]
                m = jnp.maximum(before, m)
                p = jnp.exp2(s - m[:, :1])
            else:
                p = jnp.exp2(s - m)
            o = jnp.dot(p.astype(BF16), vals, preferred_element_type=F32)
            if p0 > 0:
                fade = jnp.exp2(before - m)
                o = o + acc[i, j] * jnp.concatenate([fade, fade], axis=1)
            if last:
                out[i, :, j * HD:(j + 1) * HD] = (o[:, :HD] / o[:, HD:]).astype(BF16)
            else:
                acc[i, j] = o
                top[i, j] = jnp.broadcast_to(m, (T, HD))

    kv[0, pl.ds(IDS, 16), :] = jnp.zeros((16, CH), BF16)
    kv[0, pl.ds(IDS, 16), pl.ds(0, T)] = jnp.broadcast_to(docs[...].astype(F32), (16, T)).astype(BF16)
    kv_part(0)
    kv_final(0)
    near_start(0)
    kv_part(1)
    q_parts(2, 4)
    plane_start(0)
    q_parts(4, 6)
    kv_final(1)
    near_start(1)
    spread_start(0, 1)
    plane_on(0)
    q_parts(6, 8)
    far_start(0)
    plane_start(1)
    q_parts(8, 10)
    q_sum(9)
    spread_start(1, 1)
    spread_on(0, 1)
    plane_last(0)
    plane_on(1)
    spread_start(0, 0)
    far_start(1)
    spread_on(0, 0)
    spread_on(1, 1)
    plane_last(1)
    spread_start(1, 0)
    for f in range(2):
        for dst in (6, 7, 8):
            arrive(f, dst)
    make_bias(bias1, 0, 9)
    spread_on(1, 0)

    def first(i, c):
        q_final(i + 2)
        attend(i, 0, 9, bias1, False)
        return c

    lax.fori_loop(0, NQ, first, 0)

    @pl.when(b == 1)
    def _():
        yb_rest()

    @pl.when(b == 0)
    def _():
        ya_rest()

    make_bias(bias2, 9, 4)

    def second(i, c):
        attend(i, 9, 4, bias2, False)
        return c

    lax.fori_loop(0, NQ, second, 0)

    @pl.when(b == 0)
    def _():
        yb_rest()

    @pl.when(b == 1)
    def _():
        ya_rest()

    make_bias(bias2, 13, 4)

    def third(i, c):
        attend(i, 13, 4, bias2, True)
        return c

    lax.fori_loop(0, NQ, third, 0)

    for f in range(2):
        for far in range(2):
            if f == 1:
                tok_copy(f, far).wait_send()
        kss_copy(f).wait_send()
        ksx_copy(f).wait_send()
        for n in range(16):
            send(n, f, 0, 1, z_up).wait_send()
    t_sib.wait_send()

    def sent(i, c):
        sso_copy(i).wait_send()

        @pl.when(i > 1)
        def _():
            ssp_copy(i).wait_send()
            sx_copy(i).wait_send()

        return c

    lax.fori_loop(0, NCH, sent, 0)


def fused(tok, w, scale, cosf, sinf, docs, docs_col):
    vmem = pl.BlockSpec(memory_space=pltpu.VMEM)
    hbm = pl.BlockSpec(memory_space=pl.ANY)
    chunks = pltpu.VMEM((NCH, T, CH), BF16)
    half = pltpu.VMEM((2, H, 2 * CH), BF16)
    dma = pltpu.SemaphoreType.DMA
    return pl.pallas_call(
        fused_kernel,
        out_shape=jax.ShapeDtypeStruct((NQ, T, CH), BF16),
        in_specs=[hbm, hbm, vmem, vmem, vmem, vmem, vmem],
        out_specs=vmem,
        scratch_shapes=[
            pltpu.VMEM((NCH, SLICE, CH), BF16),
            pltpu.VMEM((2 * T, SLICE), BF16),
            pltpu.VMEM((2, T, SLICE), BF16),
            pltpu.VMEM((NCH, T, CH), F32),
            chunks, chunks, chunks, chunks, chunks, chunks, chunks,
            pltpu.VMEM((H, 2 * CH), F32),
            half, half, half, half,
            pltpu.VMEM((NPOS, BLK, CH), BF16),
            pltpu.VMEM((NQ, T, CH), BF16),
            pltpu.VMEM((NQ, PER, T, 2 * HD), F32),
            pltpu.VMEM((NQ, PER, T, HD), F32),
            pltpu.VMEM((T, FIRST * T), F32),
            pltpu.VMEM((T, 4 * T), F32),
            dma((NCH,)), dma((1,)), dma((5,)), dma((5,)),
            dma((NCH,)), dma((NCH,)), dma((NCH,)), dma((NCH,)), dma((NCH,)), dma((NCH,)),
            dma((2,)), dma((2,)), dma((2,)), dma((2,)),
            dma((2, 16)), dma((2, NPOS)),
        ],
        compiler_params=pltpu.CompilerParams(
            collective_id=0, has_side_effects=True, vmem_limit_bytes=60 << 20
        ),
        name="fused",
    )(tok, w, scale, cosf, sinf, docs, docs_col)


def local(tokens, w_qkv, col_scale, doc_ids):
    positions = lax.axis_index("ctx") * T + jnp.arange(T, dtype=jnp.int32)
    half = HD // 2
    freqs = jnp.exp(-math.log(500000.0) * 2.0 * jnp.arange(half, dtype=F32) / HD)
    angles = positions.astype(F32)[:, None] * freqs[None, :]
    cosine, sine = jnp.cos(angles), jnp.sin(angles)
    cosf = jnp.concatenate([cosine, cosine], axis=1)
    sinf = jnp.concatenate([-sine, sine], axis=1)
    out = fused(
        tokens[0], w_qkv, col_scale.reshape(NCH, 1, CH), cosf, sinf, doc_ids, doc_ids.reshape(T, 1)
    )
    return out.transpose(1, 0, 2).reshape(1, T, QH * HD)


def solution(mesh):
    return jax.shard_map(
        local,
        mesh=mesh,
        in_specs=(P("dp", "ctx", None), P("dp", None), P(), P("dp", "ctx")),
        out_specs=P("dp", "ctx", None),
        check_vma=False,
    )
```

```python
import math

import jax
import jax.numpy as jnp
from jax import lax
from jax.experimental import pallas as pl
from jax.experimental.pallas import tpu as pltpu
from jax.sharding import PartitionSpec as P

MESH = pl.DeviceIdType.MESH
QH = 32
KVH = 4
HD = 128
T = 160
H = T // 2
SLICE = 1024
CH = 512
NCH = 10
PER = CH // HD
GROUP = QH // KVH
WIDE = GROUP * T
BLK = 2 * T + 16
AT = ((0, T + 16), (T + 16, T))
IDS = T
NPOS = 17
FIRST = 9
UNROLL = 4
F32 = jnp.float32
BF16 = jnp.bfloat16
FACTOR = math.log2(math.e) / math.sqrt(HD)


def fused_kernel(
    tok, w, scale, docs,
    out,
    wv, xo, xp, po, p1, sso, rso, ssp, rsp, sx, rx, kp1, kss, krs, ksx, krx, kv, q, acc, top, tot, drow, low, cosf, sinf,
    w_sem, loc_sem, tok_s, tok_r, sso_s, sso_r, ssp_s, ssp_r, sx_s, sx_r, kss_s, kss_r, ksx_s, ksx_r, h_s, h_r,
):
    dp = lax.axis_index("dp")
    ctx = lax.axis_index("ctx")
    h = dp // 2
    k = dp % 2
    z = ctx // 8
    b = (ctx // 4) % 2
    x = ctx % 4

    def place(h_, k_, z_, b_, x_):
        return (h_ * 2 + k_, z_ * 8 + b_ * 4 + x_)

    sib = place(h, 1 - k, z, b, x)
    par = place(1 - h, k, z, 1 - b, x)
    parx = place(1 - h, 1 - k, z, 1 - b, x)
    z_up = place(h, k, (z + 1) % 8, b, x)
    z_dn = place(h, k, (z + 7) % 8, b, x)
    xi, xm, x2 = (x + 1) % 4, (x + 3) % 4, (x + 2) % 4
    d_i = place(h, k, z, b, xi)
    d_m = place(h, k, z, b, xm)
    d_2 = place(h, k, z, b, x2)
    d_y = place(h, k, z, 1 - b, x)

    def cols(i):
        return pl.ds(pl.multiple_of(((i + 8) % 10) * CH, CH), CH)

    def tok_cols(j):
        return pl.ds(pl.multiple_of(j * SLICE, SLICE), SLICE)

    def w_copy(i):
        return pltpu.make_async_copy(w.at[:, cols(i)], wv.at[i], w_sem.at[i])

    def remote(src, dst, s, r, dev):
        return pltpu.make_async_remote_copy(
            src_ref=src, dst_ref=dst, send_sem=s, recv_sem=r, device_id=dev, device_id_type=MESH
        )

    own_tok = pltpu.make_async_copy(tok.at[:, tok_cols(2 * h + k)], xo.at[pl.ds(0, T)], loc_sem.at[0])
    own_tok.start()
    for i in range(NCH):
        w_copy(i).start()

    bar = pltpu.get_barrier_semaphore()
    for dev in (sib, par, parx, z_dn, d_i, d_m, d_2, d_y):
        pl.semaphore_signal(bar, inc=1, device_id=dev, device_id_type=MESH)
    pl.semaphore_wait(bar, 8)

    def tok_copy(f, far):
        j = 2 * (1 - h) + (1 - k if far else k)
        n = 2 * f + far
        return remote(
            tok.at[pl.ds(f * H, H), tok_cols(j)], xp.at[f, pl.ds(far * H, H)], tok_s.at[n], tok_r.at[n],
            parx if far else par,
        )

    t_sib = remote(tok.at[:, tok_cols(2 * h + 1 - k)], xo.at[pl.ds(T, T)], tok_s.at[4], tok_r.at[4], sib)
    tok_copy(0, 0).start()
    tok_copy(0, 1).start()
    t_sib.start()
    own_tok.wait()
    t_sib.wait_recv()

    def sso_copy(i):
        return remote(sso.at[i], rso.at[i], sso_s.at[i], sso_r.at[i], sib)

    def ssp_copy(i):
        return remote(ssp.at[i], rsp.at[i], ssp_s.at[i], ssp_r.at[i], sib)

    def sx_copy(i):
        return remote(sx.at[i], rx.at[i], sx_s.at[i], sx_r.at[i], par)

    def kss_copy(f):
        return remote(kss.at[f], krs.at[f], kss_s.at[f], kss_r.at[f], sib)

    def ksx_copy(f):
        return remote(ksx.at[f], krx.at[f], ksx_s.at[f], ksx_r.at[f], par)

    def own_part(i, c):
        w_copy(i).wait()
        part = jnp.dot(xo[...], wv[i], preferred_element_type=F32)
        po[i] = part[:T]
        sso[i] = part[T:].astype(BF16)
        sso_copy(i).start()
        return c

    lax.fori_loop(0, 6, own_part, 0)
    for far in range(2):
        tok_copy(0, far).wait_send()
        tok_copy(1, far).start()
    lax.fori_loop(6, NCH, own_part, 0)

    def kv_part(f):
        for far in range(2):
            tok_copy(f, far).wait_recv()
        for i in range(2):
            part = jnp.dot(xp[f], wv[i], preferred_element_type=F32)
            kp1[:, i * CH:(i + 1) * CH] = part[:H]
            kss[f, :, i * CH:(i + 1) * CH] = part[H:].astype(BF16)
        kss_copy(f).start()
        kss_copy(f).wait_recv()
        ksx[f] = (kp1[...] + krs[f].astype(F32)).astype(BF16)
        ksx_copy(f).start()

    def turned(u, rows):
        return u * cosf[rows, :] + pltpu.roll(u, HD // 2, 1) * sinf[rows, :]

    def kv_final(f):
        rows = pl.ds(f * H, H)
        at = AT[f][0]
        ksx_copy(f).wait_recv()
        if f == 0:
            for i in range(2):
                sso_copy(i).wait_recv()
        u = (po[0, rows] + rso[0, rows].astype(F32) + krx[f, :, :CH].astype(F32)) * scale[:, 8 * CH:9 * CH]
        for g in range(KVH):
            kv[0, pl.ds(at, H), g * HD:(g + 1) * HD] = turned(u[:, g * HD:(g + 1) * HD], rows).astype(BF16)
        u = (po[1, rows] + rso[1, rows].astype(F32) + krx[f, :, CH:].astype(F32)) * scale[:, 9 * CH:]
        kv[0, pl.ds(at + H, H), :] = u.astype(BF16)

    def q_part(i, c):
        part = jnp.dot(xp[...].reshape(2 * T, SLICE), wv[i], preferred_element_type=F32)
        p1[i] = jnp.concatenate([part[:H], part[2 * H:3 * H]], axis=0).astype(BF16)
        ssp[i] = jnp.concatenate([part[H:2 * H], part[3 * H:]], axis=0).astype(BF16)
        ssp_copy(i).start()

        @pl.when(i > 2)
        def _():
            q_sum(i - 1)

        return c

    def q_sum(i):
        ssp_copy(i).wait_recv()
        sx[i] = (p1[i].astype(F32) + rsp[i].astype(F32)).astype(BF16)
        sx_copy(i).start()

    def q_parts(lo, hi):
        lax.fori_loop(lo, hi, q_part, 0)

    def q_final(i):
        sso_copy(i).wait_recv()
        sx_copy(i).wait_recv()
        u = (po[i] + rso[i].astype(F32) + rx[i].astype(F32)) * (scale[:, cols(i)] * FACTOR)
        heads = [turned(u[:, g * HD:(g + 1) * HD], pl.ds(0, T)) for g in range(PER)]
        at = pl.ds(pl.multiple_of((i % 2) * PER * T, PER * T), PER * T)
        q[i // 2 - 1, :, at] = jnp.concatenate(heads, axis=0).T.astype(BF16)

    yb = FIRST
    ya = FIRST + 4

    def send(n, f, src, dst, dev):
        at = pl.ds(AT[f][0], AT[f][1])
        return remote(kv.at[src, at], kv.at[dst, at], h_s.at[f, n], h_r.at[f, dst], dev)

    def arrive(f, dst):
        at = pl.ds(AT[f][0], AT[f][1])
        remote(kv.at[dst, at], kv.at[dst, at], h_s.at[f, 0], h_r.at[f, dst], sib).wait_recv()

    row = ((9, xi, 6, d_i), (10, xm, 7, d_m), (11, x2, 8, d_2))

    def near_start(f):
        send(0, f, 0, 1, z_up).start()

        @pl.when(b == 0)
        def _():
            send(12, f, 0, yb, d_y).start()

        for n, v, dst, dev in row:
            @pl.when(v > x)
            def _():
                send(n, f, 0, dst, dev).start()

    def plane_start(f):
        arrive(f, 1)
        send(1, f, 1, 2, z_up).start()
        send(2, f, 1, 3, d_i).start()
        send(3, f, 1, 4, d_m).start()

    def plane_on(f):
        arrive(f, 3)
        if f == 0:
            send(5, f, 3, 5, d_i).start()
        arrive(f, 4)
        if f == 1:
            send(5, f, 4, 5, d_m).start()

    def cross(f):
        send(4, f, 1, ya, d_y).start()

    def cross_on(f):
        send(6, f, 3, ya + 1, d_y).start()
        send(7, f, 4, ya + 2, d_y).start()

    def cross_last(f):
        arrive(f, 5)
        send(8, f, 5, ya + 3, d_y).start()

    def far_start(f):
        arrive(f, 2)

        @pl.when(b == 1)
        def _():
            send(12, f, 2, yb, d_y).start()

        for n, v, dst, dev in row:
            @pl.when(v < x)
            def _():
                send(n, f, 2, dst, dev).start()

    def spread_start(f, which):
        @pl.when(b == which)
        def _():
            arrive(f, yb)
            send(13, f, yb, yb + 1, d_i).start()
            send(14, f, yb, yb + 2, d_m).start()

    def spread_on(f, which):
        @pl.when(b == which)
        def _():
            if f == 0:
                arrive(f, yb + 2)
                send(15, f, yb + 2, yb + 3, d_m).start()
            else:
                arrive(f, yb + 1)
                send(15, f, yb + 1, yb + 3, d_i).start()

    def ya_rest():
        for r in range(4):
            for f in range(2):
                arrive(f, ya + r)

    def yb_rest():
        arrive(0, yb + 1)
        arrive(1, yb + 2)
        for f in range(2):
            arrive(f, yb + 3)

    ydist = 4 - 8 * b
    yo = jnp.where(b == 1, 4, 12)
    away = [jnp.int32(0), jnp.int32(8), jnp.int32(16), 8 + x - xm, 8 + x - xi, 8 + x - x2]
    away += [jnp.where(v < x, x - v, 16 + x - v) for v in (xm, xi, x2)]
    cross_b = [yo + x - v for v in (x, xm, xi, x2)]
    cross_a = [8 - ydist + x - v for v in (x, xm, xi, x2)]
    away += cross_b + cross_a

    def prepare():
        kv[0, pl.ds(IDS, 16), :] = jnp.zeros((16, CH), BF16)
        kv[0, pl.ds(IDS, 16), pl.ds(0, T)] = jnp.broadcast_to(docs[...].astype(F32), (16, T)).astype(BF16)
        for j in range(GROUP):
            drow[:, j * T:(j + 1) * T] = docs[...].astype(F32)
        lane = lax.broadcasted_iota(jnp.int32, (T, HD), 1)
        i = jnp.where(lane < HD // 2, lane, lane - HD // 2).astype(F32)
        freq = jnp.exp(-math.log(500000.0) * 2.0 * i / HD)
        pos = ctx * T + lax.broadcasted_iota(jnp.int32, (T, HD), 0)
        angle = pos.astype(F32) * freq
        cosf[...] = jnp.cos(angle)
        sine = jnp.sin(angle)
        sinf[...] = jnp.where(lane < HD // 2, -sine, sine)

    def make_low(p0, n):
        doc = lax.broadcasted_iota(jnp.int32, (8, 1), 0).astype(F32)
        mine = (drow[...] == doc).astype(F32)
        for p in range(p0, p0 + n):
            ids = kv[p, pl.ds(IDS, 16), :][0:1, 0:T].astype(F32)
            count = jnp.sum((ids < doc).astype(F32), axis=1, keepdims=True)
            count = jnp.where(ctx >= away[p], count, float(T))
            low[p] = jnp.sum(mine * count, axis=0, keepdims=True)

    def attend(g, p0, n, last):
        lanes = pl.ds(pl.multiple_of(g * HD, HD), HD)
        where = pl.ds(p0, n)

        def rows(lo):
            parts = [kv[where, pl.ds(AT[f][0] + lo, H), lanes].reshape(n * H, HD) for f in range(2)]
            return jnp.concatenate(parts, axis=0)

        s = jnp.dot(rows(0), q[g], preferred_element_type=F32)
        r = lax.broadcasted_iota(jnp.int32, (H, WIDE), 0).astype(F32)
        parts = []
        for f in range(2):
            for i in range(n):
                keep = r >= low[p0 + i] - f * H
                if p0 + i == 0:
                    t = lax.broadcasted_iota(jnp.int32, (1, WIDE), 1).astype(F32)
                    t = t - T * jnp.floor((t + 0.5) / T)
                    keep = keep & (r <= t - f * H)
                at = (f * n + i) * H
                parts.append(jnp.where(keep, s[at:at + H], -jnp.inf))
        s = jnp.concatenate(parts, axis=0)
        m = jnp.max(s, axis=0, keepdims=True)
        if p0 > 0:
            before = top[g, 0:1]
            m = jnp.maximum(before, m)
        p = jnp.exp2(s - m)
        total = jnp.sum(p, axis=0, keepdims=True)
        o = lax.dot_general(rows(H), p.astype(BF16), (((0,), (0,)), ((), ())), preferred_element_type=F32)
        if p0 > 0:
            fade = jnp.exp2(before - m)
            o = o + acc[g] * fade
            total = total + tot[g, 0:1] * fade
        if last:
            o = (o / total).T.astype(BF16)
            for j in range(GROUP):
                at = pl.multiple_of((g * GROUP + j) * HD, HD)
                out[:, pl.ds(at, HD)] = o[j * T:(j + 1) * T]
        else:
            acc[g] = o
            top[g] = jnp.broadcast_to(m, (8, WIDE))
            tot[g] = jnp.broadcast_to(total, (8, WIDE))

    kv_part(0)
    prepare()
    kv_final(0)
    near_start(0)
    kv_part(1)
    q_parts(2, 4)
    plane_start(0)
    cross(0)
    q_parts(4, 6)
    kv_final(1)
    near_start(1)
    spread_start(0, 1)
    plane_on(0)
    far_start(0)
    cross_on(0)
    q_parts(6, 8)
    plane_start(1)
    spread_start(1, 1)
    q_parts(8, 10)
    q_sum(9)
    spread_on(0, 1)
    cross_last(0)
    spread_start(0, 0)
    plane_on(1)
    far_start(1)
    cross(1)
    cross_on(1)
    spread_on(0, 0)
    spread_on(1, 1)
    cross_last(1)

    def first(g, c):
        q_final(2 * g + 2)
        q_final(2 * g + 3)
        attend(g, 0, 6, False)
        return c

    make_low(0, 6)
    lax.fori_loop(0, 1, first, 0)
    spread_start(1, 0)
    lax.fori_loop(1, 2, first, 0)
    spread_on(1, 0)
    lax.fori_loop(2, KVH, first, 0)
    for f in range(2):
        for dst in (6, 7, 8):
            arrive(f, dst)

    yb_rest()
    make_low(6, 7)

    def second(g, c):
        attend(g, 6, 7, False)
        return c

    lax.fori_loop(0, KVH, second, 0, unroll=UNROLL)

    ya_rest()
    make_low(13, 4)

    def third(g, c):
        attend(g, 13, 4, True)
        return c

    lax.fori_loop(0, KVH, third, 0, unroll=UNROLL)

    for f in range(2):
        for far in range(2):
            if f == 1:
                tok_copy(f, far).wait_send()
        kss_copy(f).wait_send()
        ksx_copy(f).wait_send()
        for n in range(16):
            send(n, f, 0, 1, z_up).wait_send()
    t_sib.wait_send()

    def sent(i, c):
        sso_copy(i).wait_send()

        @pl.when(i > 1)
        def _():
            ssp_copy(i).wait_send()
            sx_copy(i).wait_send()

        return c

    lax.fori_loop(0, NCH, sent, 0)


def fused(tok, w, scale, docs):
    vmem = pl.BlockSpec(memory_space=pltpu.VMEM)
    hbm = pl.BlockSpec(memory_space=pl.ANY)
    chunks = pltpu.VMEM((NCH, T, CH), BF16)
    half = pltpu.VMEM((2, H, 2 * CH), BF16)
    dma = pltpu.SemaphoreType.DMA
    return pl.pallas_call(
        fused_kernel,
        out_shape=jax.ShapeDtypeStruct((T, QH * HD), BF16),
        in_specs=[hbm, hbm, vmem, vmem],
        out_specs=vmem,
        scratch_shapes=[
            pltpu.VMEM((NCH, SLICE, CH), BF16),
            pltpu.VMEM((2 * T, SLICE), BF16),
            pltpu.VMEM((2, T, SLICE), BF16),
            pltpu.VMEM((NCH, T, CH), F32),
            chunks, chunks, chunks, chunks, chunks, chunks, chunks,
            pltpu.VMEM((H, 2 * CH), F32),
            half, half, half, half,
            pltpu.VMEM((NPOS, BLK, CH), BF16),
            pltpu.VMEM((KVH, HD, WIDE), BF16),
            pltpu.VMEM((KVH, HD, WIDE), F32),
            pltpu.VMEM((KVH, 8, WIDE), F32),
            pltpu.VMEM((KVH, 8, WIDE), F32),
            pltpu.VMEM((1, WIDE), F32),
            pltpu.VMEM((NPOS, 1, WIDE), F32),
            pltpu.VMEM((T, HD), F32),
            pltpu.VMEM((T, HD), F32),
            dma((NCH,)), dma((1,)), dma((5,)), dma((5,)),
            dma((NCH,)), dma((NCH,)), dma((NCH,)), dma((NCH,)), dma((NCH,)), dma((NCH,)),
            dma((2,)), dma((2,)), dma((2,)), dma((2,)),
            dma((2, 16)), dma((2, NPOS)),
        ],
        compiler_params=pltpu.CompilerParams(
            collective_id=0, has_side_effects=True, vmem_limit_bytes=60 << 20
        ),
        name="fused",
    )(tok, w, scale, docs)


def local(tokens, w_qkv, col_scale, doc_ids):
    return fused(tokens[0], w_qkv, col_scale.reshape(1, -1), doc_ids)[None]


def solution(mesh):
    return jax.shard_map(
        local,
        mesh=mesh,
        in_specs=(P("dp", "ctx", None), P("dp", None), P(), P("dp", "ctx")),
        out_specs=P("dp", "ctx", None),
        check_vma=False,
    )
```

```python
import math

import jax
import jax.numpy as jnp
from jax import lax
from jax.experimental import pallas as pl
from jax.experimental.pallas import tpu as pltpu
from jax.sharding import PartitionSpec as P

MESH = pl.DeviceIdType.MESH
QH = 32
KVH = 4
HD = 128
T = 160
H = T // 2
SLICE = 1024
CH = 512
NCH = 10
PER = CH // HD
GROUP = QH // KVH
WIDE = GROUP * T
BLK = 2 * T + 16
AT = ((0, T + 16), (T + 16, T))
IDS = T
NPOS = 17
FIRST = 9
UNROLL = 4
F32 = jnp.float32
BF16 = jnp.bfloat16
FACTOR = math.log2(math.e) / math.sqrt(HD)


def fused_kernel(
    tok, w, scale, docs,
    out,
    wv, xo, xp, po, p1, sso, rso, ssp, rsp, sx, rx, kp1, kss, krs, ksx, krx, kv, q, acc, top, tot, drow, low, cosf, sinf,
    w_sem, loc_sem, tok_s, tok_r, sso_s, sso_r, ssp_s, ssp_r, sx_s, sx_r, kss_s, kss_r, ksx_s, ksx_r, h_s, h_r,
):
    dp = lax.axis_index("dp")
    ctx = lax.axis_index("ctx")
    h = dp // 2
    k = dp % 2
    z = ctx // 8
    b = (ctx // 4) % 2
    x = ctx % 4

    def place(h_, k_, z_, b_, x_):
        return (h_ * 2 + k_, z_ * 8 + b_ * 4 + x_)

    sib = place(h, 1 - k, z, b, x)
    par = place(1 - h, k, z, 1 - b, x)
    parx = place(1 - h, 1 - k, z, 1 - b, x)
    z_up = place(h, k, (z + 1) % 8, b, x)
    z_dn = place(h, k, (z + 7) % 8, b, x)
    xi, xm, x2 = (x + 1) % 4, (x + 3) % 4, (x + 2) % 4
    d_i = place(h, k, z, b, xi)
    d_m = place(h, k, z, b, xm)
    d_2 = place(h, k, z, b, x2)
    d_y = place(h, k, z, 1 - b, x)

    def cols(i):
        return pl.ds(pl.multiple_of(((i + 8) % 10) * CH, CH), CH)

    def tok_cols(j):
        return pl.ds(pl.multiple_of(j * SLICE, SLICE), SLICE)

    def w_copy(i):
        return pltpu.make_async_copy(w.at[:, cols(i)], wv.at[i], w_sem.at[i])

    def remote(src, dst, s, r, dev):
        return pltpu.make_async_remote_copy(
            src_ref=src, dst_ref=dst, send_sem=s, recv_sem=r, device_id=dev, device_id_type=MESH
        )

    own_tok = pltpu.make_async_copy(tok.at[:, tok_cols(2 * h + k)], xo.at[pl.ds(0, T)], loc_sem.at[0])
    own_tok.start()
    for i in range(NCH):
        w_copy(i).start()

    bar = pltpu.get_barrier_semaphore()
    for dev in (sib, par, parx, z_dn, d_i, d_m, d_2, d_y):
        pl.semaphore_signal(bar, inc=1, device_id=dev, device_id_type=MESH)
    pl.semaphore_wait(bar, 8)

    def tok_copy(f, far):
        j = 2 * (1 - h) + (1 - k if far else k)
        n = 2 * f + far
        return remote(
            tok.at[pl.ds(f * H, H), tok_cols(j)], xp.at[f, pl.ds(far * H, H)], tok_s.at[n], tok_r.at[n],
            parx if far else par,
        )

    t_sib = remote(tok.at[:, tok_cols(2 * h + 1 - k)], xo.at[pl.ds(T, T)], tok_s.at[4], tok_r.at[4], sib)
    tok_copy(0, 0).start()
    tok_copy(0, 1).start()
    t_sib.start()
    own_tok.wait()
    t_sib.wait_recv()

    def sso_copy(i):
        return remote(sso.at[i], rso.at[i], sso_s.at[i], sso_r.at[i], sib)

    def ssp_copy(i):
        return remote(ssp.at[i], rsp.at[i], ssp_s.at[i], ssp_r.at[i], sib)

    def sx_copy(i):
        return remote(sx.at[i], rx.at[i], sx_s.at[i], sx_r.at[i], par)

    def kss_copy(f):
        return remote(kss.at[f], krs.at[f], kss_s.at[f], kss_r.at[f], sib)

    def ksx_copy(f):
        return remote(ksx.at[f], krx.at[f], ksx_s.at[f], ksx_r.at[f], par)

    def own_part(i, c):
        w_copy(i).wait()
        part = jnp.dot(xo[...], wv[i], preferred_element_type=F32)
        po[i] = part[:T]
        sso[i] = part[T:].astype(BF16)
        sso_copy(i).start()
        return c

    lax.fori_loop(0, 6, own_part, 0)
    for far in range(2):
        tok_copy(0, far).wait_send()
        tok_copy(1, far).start()
    lax.fori_loop(6, NCH, own_part, 0)

    def kv_part(f):
        for far in range(2):
            tok_copy(f, far).wait_recv()
        for i in range(2):
            part = jnp.dot(xp[f], wv[i], preferred_element_type=F32)
            kp1[:, i * CH:(i + 1) * CH] = part[:H]
            kss[f, :, i * CH:(i + 1) * CH] = part[H:].astype(BF16)
        kss_copy(f).start()
        kss_copy(f).wait_recv()
        ksx[f] = (kp1[...] + krs[f].astype(F32)).astype(BF16)
        ksx_copy(f).start()

    def turned(u, rows):
        return u * cosf[rows, :] + pltpu.roll(u, HD // 2, 1) * sinf[rows, :]

    def kv_final(f):
        rows = pl.ds(f * H, H)
        at = AT[f][0]
        ksx_copy(f).wait_recv()
        if f == 0:
            for i in range(2):
                sso_copy(i).wait_recv()
        u = (po[0, rows] + rso[0, rows].astype(F32) + krx[f, :, :CH].astype(F32)) * scale[:, 8 * CH:9 * CH]
        for g in range(KVH):
            kv[0, pl.ds(at, H), g * HD:(g + 1) * HD] = turned(u[:, g * HD:(g + 1) * HD], rows).astype(BF16)
        u = (po[1, rows] + rso[1, rows].astype(F32) + krx[f, :, CH:].astype(F32)) * scale[:, 9 * CH:]
        kv[0, pl.ds(at + H, H), :] = u.astype(BF16)

    def q_part(i, c):
        part = jnp.dot(xp[...].reshape(2 * T, SLICE), wv[i], preferred_element_type=F32)
        p1[i] = jnp.concatenate([part[:H], part[2 * H:3 * H]], axis=0).astype(BF16)
        ssp[i] = jnp.concatenate([part[H:2 * H], part[3 * H:]], axis=0).astype(BF16)
        ssp_copy(i).start()

        @pl.when(i > 2)
        def _():
            q_sum(i - 1)

        return c

    def q_sum(i):
        ssp_copy(i).wait_recv()
        sx[i] = (p1[i].astype(F32) + rsp[i].astype(F32)).astype(BF16)
        sx_copy(i).start()

    def q_parts(lo, hi):
        lax.fori_loop(lo, hi, q_part, 0)

    def q_final(i):
        sso_copy(i).wait_recv()
        sx_copy(i).wait_recv()
        u = (po[i] + rso[i].astype(F32) + rx[i].astype(F32)) * (scale[:, cols(i)] * FACTOR)
        heads = [turned(u[:, g * HD:(g + 1) * HD], pl.ds(0, T)) for g in range(PER)]
        at = pl.ds((i % 2) * PER * T, PER * T)
        q[i // 2 - 1, :, at] = jnp.concatenate(heads, axis=0).T.astype(BF16)

    yb = FIRST
    ya = FIRST + 4

    def send(n, f, src, dst, dev):
        at = pl.ds(AT[f][0], AT[f][1])
        return remote(kv.at[src, at], kv.at[dst, at], h_s.at[f, n], h_r.at[f, dst], dev)

    def arrive(f, dst):
        at = pl.ds(AT[f][0], AT[f][1])
        remote(kv.at[dst, at], kv.at[dst, at], h_s.at[f, 0], h_r.at[f, dst], sib).wait_recv()

    row = ((9, xi, 6, d_i), (10, xm, 7, d_m), (11, x2, 8, d_2))

    def near_start(f):
        send(0, f, 0, 1, z_up).start()

        @pl.when(b == 0)
        def _():
            send(12, f, 0, yb, d_y).start()

        for n, v, dst, dev in row:
            @pl.when(v > x)
            def _():
                send(n, f, 0, dst, dev).start()

    def plane_start(f):
        arrive(f, 1)
        send(1, f, 1, 2, z_up).start()
        send(2, f, 1, 3, d_i).start()
        send(3, f, 1, 4, d_m).start()

    def plane_on(f):
        arrive(f, 3)
        if f == 0:
            send(5, f, 3, 5, d_i).start()
        arrive(f, 4)
        if f == 1:
            send(5, f, 4, 5, d_m).start()

    def cross(f):
        send(4, f, 1, ya, d_y).start()

    def cross_on(f):
        send(6, f, 3, ya + 1, d_y).start()
        send(7, f, 4, ya + 2, d_y).start()

    def cross_last(f):
        arrive(f, 5)
        send(8, f, 5, ya + 3, d_y).start()

    def far_start(f):
        arrive(f, 2)

        @pl.when(b == 1)
        def _():
            send(12, f, 2, yb, d_y).start()

        for n, v, dst, dev in row:
            @pl.when(v < x)
            def _():
                send(n, f, 2, dst, dev).start()

    def spread_start(f, which):
        @pl.when(b == which)
        def _():
            arrive(f, yb)
            send(13, f, yb, yb + 1, d_i).start()
            send(14, f, yb, yb + 2, d_m).start()

    def spread_on(f, which):
        @pl.when(b == which)
        def _():
            if f == 0:
                arrive(f, yb + 2)
                send(15, f, yb + 2, yb + 3, d_m).start()
            else:
                arrive(f, yb + 1)
                send(15, f, yb + 1, yb + 3, d_i).start()

    def ya_rest():
        for r in range(4):
            for f in range(2):
                arrive(f, ya + r)

    def yb_rest():
        arrive(0, yb + 1)
        arrive(1, yb + 2)
        for f in range(2):
            arrive(f, yb + 3)

    ydist = 4 - 8 * b
    yo = jnp.where(b == 1, 4, 12)
    away = [jnp.int32(0), jnp.int32(8), jnp.int32(16), 8 + x - xm, 8 + x - xi, 8 + x - x2]
    away += [jnp.where(v < x, x - v, 16 + x - v) for v in (xm, xi, x2)]
    cross_b = [yo + x - v for v in (x, xm, xi, x2)]
    cross_a = [8 - ydist + x - v for v in (x, xm, xi, x2)]
    away += cross_b + cross_a

    def prepare():
        kv[0, pl.ds(IDS, 16), :] = jnp.zeros((16, CH), BF16)
        kv[0, pl.ds(IDS, 16), pl.ds(0, T)] = jnp.broadcast_to(docs[...].astype(F32), (16, T)).astype(BF16)
        for j in range(GROUP):
            drow[:, j * T:(j + 1) * T] = docs[...].astype(F32)
        lane = lax.broadcasted_iota(jnp.int32, (T, HD), 1)
        i = jnp.where(lane < HD // 2, lane, lane - HD // 2).astype(F32)
        freq = jnp.exp(-math.log(500000.0) * 2.0 * i / HD)
        pos = ctx * T + lax.broadcasted_iota(jnp.int32, (T, HD), 0)
        angle = pos.astype(F32) * freq
        cosf[...] = jnp.cos(angle)
        sine = jnp.sin(angle)
        sinf[...] = jnp.where(lane < HD // 2, -sine, sine)

    def make_low(p0, n):
        doc = lax.broadcasted_iota(jnp.int32, (8, 1), 0).astype(F32)
        mine = (drow[...] == doc).astype(F32)
        for p in range(p0, p0 + n):
            ids = kv[p, pl.ds(IDS, 16), :][0:1, 0:T].astype(F32)
            count = jnp.sum((ids < doc).astype(F32), axis=1, keepdims=True)
            count = jnp.where(ctx >= away[p], count, float(T))
            low[p] = jnp.sum(mine * count, axis=0, keepdims=True)

    def attend(g, p0, n, last):
        lanes = pl.ds(g * HD if isinstance(g, int) else pl.multiple_of(g * HD, HD), HD)
        where = pl.ds(p0, n)

        def rows(lo):
            parts = [kv[where, pl.ds(AT[f][0] + lo, H), lanes].reshape(n * H, HD) for f in range(2)]
            return jnp.concatenate(parts, axis=0)

        s = jnp.dot(rows(0), q[g], preferred_element_type=F32)
        r = lax.broadcasted_iota(jnp.int32, (H, WIDE), 0).astype(F32)
        parts = []
        for f in range(2):
            for i in range(n):
                keep = r >= low[p0 + i] - f * H
                if p0 + i == 0:
                    t = lax.broadcasted_iota(jnp.int32, (1, WIDE), 1).astype(F32)
                    t = t - T * jnp.floor((t + 0.5) / T)
                    keep = keep & (r <= t - f * H)
                at = (f * n + i) * H
                parts.append(jnp.where(keep, s[at:at + H], -jnp.inf))
        s = jnp.concatenate(parts, axis=0)
        m = jnp.max(s, axis=0, keepdims=True)
        if p0 > 0:
            before = top[g, 0:1]
            m = jnp.maximum(before, m)
        p = jnp.exp2(s - m)
        total = jnp.sum(p, axis=0, keepdims=True)
        o = lax.dot_general(rows(H), p.astype(BF16), (((0,), (0,)), ((), ())), preferred_element_type=F32)
        if p0 > 0:
            fade = jnp.exp2(before - m)
            o = o + acc[g] * fade
            total = total + tot[g, 0:1] * fade
        if last:
            o = (o / total).T.astype(BF16)
            for j in range(GROUP):
                at = pl.multiple_of((g * GROUP + j) * HD, HD)
                out[:, pl.ds(at, HD)] = o[j * T:(j + 1) * T]
        else:
            acc[g] = o
            top[g] = jnp.broadcast_to(m, (8, WIDE))
            tot[g] = jnp.broadcast_to(total, (8, WIDE))

    kv_part(0)
    prepare()
    kv_final(0)
    near_start(0)
    kv_part(1)
    q_parts(2, 4)
    plane_start(0)
    cross(0)
    q_parts(4, 6)
    kv_final(1)
    near_start(1)
    spread_start(0, 1)
    plane_on(0)
    far_start(0)
    cross_on(0)
    q_parts(6, 8)
    plane_start(1)
    spread_start(1, 1)
    q_parts(8, 10)
    q_sum(9)
    spread_on(0, 1)
    cross_last(0)
    q_final(2)
    spread_start(0, 0)
    plane_on(1)
    q_final(3)
    far_start(1)
    cross(1)
    cross_on(1)
    q_final(4)
    spread_on(0, 0)
    spread_on(1, 1)
    cross_last(1)
    q_final(5)
    make_low(0, 6)
    attend(0, 0, 6, False)
    spread_start(1, 0)
    attend(1, 0, 6, False)
    q_final(6)
    spread_on(1, 0)
    q_final(7)
    for f in range(2):
        for dst in (6, 7, 8):
            arrive(f, dst)
    make_low(6, 3)
    attend(2, 0, 9, False)
    attend(0, 6, 3, False)
    attend(1, 6, 3, False)
    q_final(8)
    q_final(9)
    attend(3, 0, 9, False)
    yb_rest()
    make_low(9, 4)

    def second(g, c):
        attend(g, 9, 4, False)
        return c

    lax.fori_loop(0, KVH, second, 0, unroll=UNROLL)

    ya_rest()
    make_low(13, 4)

    def third(g, c):
        attend(g, 13, 4, True)
        return c

    lax.fori_loop(0, KVH, third, 0, unroll=UNROLL)

    for f in range(2):
        for far in range(2):
            if f == 1:
                tok_copy(f, far).wait_send()
        kss_copy(f).wait_send()
        ksx_copy(f).wait_send()
        for n in range(16):
            send(n, f, 0, 1, z_up).wait_send()
    t_sib.wait_send()

    def sent(i, c):
        sso_copy(i).wait_send()

        @pl.when(i > 1)
        def _():
            ssp_copy(i).wait_send()
            sx_copy(i).wait_send()

        return c

    lax.fori_loop(0, NCH, sent, 0)


def fused(tok, w, scale, docs):
    vmem = pl.BlockSpec(memory_space=pltpu.VMEM)
    hbm = pl.BlockSpec(memory_space=pl.ANY)
    chunks = pltpu.VMEM((NCH, T, CH), BF16)
    half = pltpu.VMEM((2, H, 2 * CH), BF16)
    dma = pltpu.SemaphoreType.DMA
    return pl.pallas_call(
        fused_kernel,
        out_shape=pltpu.VMEM((T, QH * HD), BF16),
        in_specs=[hbm, hbm, vmem, vmem],
        out_specs=vmem,
        scratch_shapes=[
            pltpu.VMEM((NCH, SLICE, CH), BF16),
            pltpu.VMEM((2 * T, SLICE), BF16),
            pltpu.VMEM((2, T, SLICE), BF16),
            pltpu.VMEM((NCH, T, CH), F32),
            chunks, chunks, chunks, chunks, chunks, chunks, chunks,
            pltpu.VMEM((H, 2 * CH), F32),
            half, half, half, half,
            pltpu.VMEM((NPOS, BLK, CH), BF16),
            pltpu.VMEM((KVH, HD, WIDE), BF16),
            pltpu.VMEM((KVH, HD, WIDE), F32),
            pltpu.VMEM((KVH, 8, WIDE), F32),
            pltpu.VMEM((KVH, 8, WIDE), F32),
            pltpu.VMEM((1, WIDE), F32),
            pltpu.VMEM((NPOS, 1, WIDE), F32),
            pltpu.VMEM((T, HD), F32),
            pltpu.VMEM((T, HD), F32),
            dma((NCH,)), dma((1,)), dma((5,)), dma((5,)),
            dma((NCH,)), dma((NCH,)), dma((NCH,)), dma((NCH,)), dma((NCH,)), dma((NCH,)),
            dma((2,)), dma((2,)), dma((2,)), dma((2,)),
            dma((2, 16)), dma((2, NPOS)),
        ],
        compiler_params=pltpu.CompilerParams(
            collective_id=0, has_side_effects=True, vmem_limit_bytes=57 << 20
        ),
        name="fused",
    )(tok, w, scale, docs)


def local(tokens, w_qkv, col_scale, doc_ids):
    return fused(tokens[0], w_qkv, col_scale.reshape(1, -1), doc_ids)[None]


def solution(mesh):
    return jax.shard_map(
        local,
        mesh=mesh,
        in_specs=(P("dp", "ctx", None), P("dp", None), P(), P("dp", "ctx")),
        out_specs=P("dp", "ctx", None),
        check_vma=False,
    )
```
